256 devices in a mesh: replica: 8 (over y, z_hi), fsdp: 32 (over x, z_lo, core).
Axes of the slice: x: 4, y: 4, z: 8 (z_hi: 2, z_lo: 4; z = z_hi * 4 + z_lo), core: 2. Of those that a mesh axis runs over, the one named last changes fastest.
Arguments:
- activations: bfloat16 [8, 4096, 8192], P('replica', 'fsdp'), may hold values from -6 to 6
- cotangent: bfloat16 [8, 4096, 1024], P('replica', 'fsdp'), may hold values from -12 to 12
- weight: float32 [8, 8192, 1024], P('replica', 'fsdp'), may hold values from -6 to 6
- moment: float32 [8, 8192, 1024], P('replica', 'fsdp'), may hold values from -6 to 6
- variance: float32 [8, 8192, 1024], P('replica', 'fsdp'), may hold values from 0.5 to 8
- outer_frag: float32 [8192, 128], P('fsdp'), may hold values from -6 to 6
- outer_mom: float32 [8192, 128], P('fsdp'), may hold values from -6 to 6
- fragment: int32 [1], replicated, may hold values from 0 to 7
Outputs:
- projected: bfloat16 [8, 4096, 1024], P('replica', 'fsdp')
- input_cotangent: bfloat16 [8, 4096, 8192], P('replica', 'fsdp')
- new_weight: float32 [8, 8192, 1024], P('replica', 'fsdp')
- new_moment: float32 [8, 8192, 1024], P('replica', 'fsdp')
- new_variance: float32 [8, 8192, 1024], P('replica', 'fsdp')
- new_outer: float32 [8192, 128], P('fsdp')
- new_momentum: float32 [8192, 128], P('fsdp')
The draws below stay inside these ranges and needn't reach their ends.
All inputs are finite; a program needn't handle non-finite values.
Results may differ from the reference program's by a relative error of at most 0.0054.
Values may be sent and summed in bfloat16 or wider, within the bound.
A program may use at most 128 MiB of HBM per device.

```python
import math
import jax
import jax.numpy as jnp
from jax import lax

D = 8192
HEADS = 8
HD = 128
KW = 1024
TOKENS = 4096
REPLICAS = 8
N_REPLICA = 8


def spiked(array, rng, source, target, parts, factor):
    owner, partner = [(jnp.arange(array.shape[position]) // (array.shape[position] // parts)).reshape([-1 if axis == position else 1 for axis in range(array.ndim)]) for position in (source, target)]
    chosen = jax.random.permutation(rng, parts)[partner]
    strong = (owner == chosen) | (owner == (partner + parts // 2) % parts)
    return jnp.where(strong, factor * array, array)


def levels(stream_key, extent, shards, least, top_value):
    level, own = 1.0, jax.random.fold_in(stream_key, 6)
    for dim, blocks in shards:
        draws = jnp.exp(jax.random.uniform(jax.random.fold_in(own, dim), (blocks,), jnp.float32, least / len(shards), top_value / len(shards)))
        level = level * jnp.repeat(draws, extent[dim] // blocks).reshape([-1 if axis == dim else 1 for axis in range(len(extent))])
    return level


def normal_values(rng, extent, scale, limit, shards=(), held_as=jnp.bfloat16):
    drawn = scale * jax.random.normal(rng, extent, jnp.float32)
    if shards:
        drawn = drawn * levels(rng, extent, shards, -0.22, 0.18)
    return jnp.clip(drawn, -limit, limit).astype(held_as)


def gaussian_with(stream_key, dims, spread, limit, split, heavy, held_as=jnp.bfloat16):
    array = spread * jax.random.normal(stream_key, dims, jnp.float32)
    if split:
        array = array * levels(stream_key, dims, split, -0.22, 0.18)
    return jnp.clip(spiked(array, jax.random.fold_in(stream_key, 3), *heavy), -limit, limit).astype(held_as)


def setup_inputs(seed: int = 0) -> dict:
    key_of = jax.random.split(jax.random.key(seed), 9)
    activations = gaussian_with(key_of[0], (REPLICAS, TOKENS, D), 1.0, 6.0, ((0, 8), (1, 32)), (1, 2, 32, 2.75))
    cotangent = normal_values(key_of[1], (REPLICAS, TOKENS, KW), 2.0, 12.0, ((0, 8), (1, 32)))
    weight = normal_values(key_of[2], (REPLICAS, D, KW), 1.0, 6.0, ((0, 8), (1, 32)), jnp.float32)
    moment = normal_values(key_of[3], (REPLICAS, D, KW), 1.0, 6.0, ((0, 8), (1, 32)), jnp.float32)
    variance = jnp.clip(jnp.exp(math.log(8.0) - 2.7725887 * jax.random.uniform(key_of[4], (REPLICAS, D, KW), jnp.float32) ** levels(key_of[4], (REPLICAS, D, KW), ((0, 8), (1, 32)), -0.2, 0.2)), 0.5, 8.0)
    outer_frag = normal_values(key_of[5], (D, HD), 1.0, 6.0, ((0, 32),), jnp.float32)
    outer_mom = normal_values(key_of[6], (D, HD), 1.0, 6.0, ((0, 32),), jnp.float32)
    fragment = jax.random.randint(key_of[7], (1,), 0, HEADS).astype(jnp.int32)
    return {"activations": activations, "cotangent": cotangent, "weight": weight, "moment": moment, "variance": variance, "outer_frag": outer_frag, "outer_mom": outer_mom, "fragment": fragment}


beta_first = 0.9
beta_second = 0.95
inner_rate = 0.1
decay_rate = 0.1
epsilon = 1e-08
outer_rate = 0.7
outer_beta = 0.9
mixing = 0.5

def reference(activations, cotangent, weight, moment, variance, outer_frag, outer_mom, fragment):
    scale = float(D) ** (-0.5)
    column_start = (fragment[0] * HD).astype(jnp.int32)
    zero_index = jnp.zeros((), jnp.int32)

    def replica_step(items):
        inputs, upstream, local, first, second = items
        cast = local.astype(jnp.bfloat16)
        projected = (jnp.dot(inputs, cast, preferred_element_type=jnp.float32) * scale).astype(jnp.bfloat16)
        backward = (lax.dot_general(upstream, cast, (((1,), (1,)), ((), ())), preferred_element_type=jnp.float32) * scale).astype(jnp.bfloat16)
        gradient = lax.dot_general(inputs, upstream, (((0,), (0,)), ((), ())), preferred_element_type=jnp.float32) * scale
        first_new = beta_first * first + (1.0 - beta_first) * gradient
        second_new = beta_second * second + (1.0 - beta_second) * gradient * gradient
        stepped = local - inner_rate * (first_new / (jnp.sqrt(second_new) + epsilon) + decay_rate * local)
        delta = outer_frag - lax.dynamic_slice(local, (zero_index, column_start), (D, HD))
        return (projected, backward, stepped, first_new, second_new, delta)
    projected, backward, stepped, first_new, second_new, delta = lax.map(replica_step, (activations, cotangent, weight, moment, variance))
    average = lax.optimization_barrier(jnp.sum(delta, axis=0)) / float(N_REPLICA)
    new_momentum = outer_beta * outer_mom + average
    new_outer = outer_frag - outer_rate * (average + outer_beta * new_momentum)
    current = lax.dynamic_slice(stepped, (zero_index, zero_index, column_start), (stepped.shape[0], D, HD))
    merged = mixing * current + (1.0 - mixing) * new_outer[None]
    new_weight = lax.dynamic_update_slice(stepped, merged, (zero_index, zero_index, column_start))
    return (projected, backward, new_weight, first_new, second_new, new_outer, new_momentum)
```

```python
import functools

import jax
import jax.numpy as jnp
from jax import lax
from jax.experimental import pallas as pl
from jax.experimental.pallas import tpu as pltpu
from jax.sharding import PartitionSpec as P

MESH = pl.DeviceIdType.MESH

D = 8192
HD = 128
KW = 1024
TOK = 128
ROWS = 256
SCALE = float(D) ** (-0.5)

beta_first = 0.9
beta_second = 0.95
inner_rate = 0.1
decay_rate = 0.1
epsilon = 1e-08
outer_rate = 0.7
outer_beta = 0.9
mixing = 0.5

F32 = jnp.float32
BF16 = jnp.bfloat16


def step_kernel(
    frag, a_in, c_in, w_in, m_in, v_in, of_in, om_in,
    proj_out, dx_out, nw_out, nm_out, nv_out, no_out, nmom_out,
    acts, cots, wall, wv, mv, vv, ofv, omv, delta, total, gblk, gsend, g_oi, g_ii, g_io,
    part, part_in, psend, p_in, pv, dxs, y_in, zsum, z_in,
    load_sem, own_sem, out_sem, w_send, w_recv, c_send, c_recv, cf_send, cf_recv,
    a_send, a_recv, g_send, oi_recv, ii_recv, io_recv, pc_send, pc_recv, px_send, px_recv,
    dx_send, dx_recv, dx_own, ys_send, ys_recv, zs_send, zs_recv, yg_send, yg_recv,
):
    rep = lax.axis_index("replica")
    fs = lax.axis_index("fsdp")
    y, zh = rep // 2, rep % 2
    x, z, c = fs // 8, (fs // 2) % 4, fs % 2
    t = x * 2 + c
    hi = z // 2
    inner = hi + (z % 2) - 2 * hi * (z % 2)
    p = z + 1 - 2 * (z % 2)
    q = 3 - z
    r = 3 - p

    def at(xx, zz, cc):
        return (rep, xx * 8 + zz * 2 + cc)

    def group(i):
        u = (t + i) % 8
        return u // 2, u % 2

    def other_x(i):
        return (x + i) % 4

    def from_x(i):
        return (x + 4 - i) % 4

    def rep_at(yy, hh):
        return (yy * 2 + hh, fs)

    def remote(src, dst, send, recv, device):
        return pltpu.make_async_remote_copy(
            src_ref=src, dst_ref=dst, send_sem=send, recv_sem=recv, device_id=device, device_id_type=MESH
        )

    def wait_bytes(ref, sem):
        pltpu.make_async_copy(ref, ref, sem).wait()

    order = (q + inner * (r - q), r + inner * (p - r), p + inner * (q - p), z)

    def column(xx, zz, cc):
        return pl.multiple_of(xx * 2048 + zz * 512 + cc * 256, 256)

    def own_rows(index):
        return pl.ds(pl.multiple_of(index * TOK, TOK), TOK)

    load_w = pltpu.make_async_copy(w_in, wv, load_sem.at[0])
    load_of = pltpu.make_async_copy(of_in, ofv, load_sem.at[1])
    load_c = pltpu.make_async_copy(c_in, cots.at[own_rows(t), :], load_sem.at[2])
    load_om = pltpu.make_async_copy(om_in, omv, load_sem.at[3])
    load_m = pltpu.make_async_copy(m_in, mv, load_sem.at[4])
    load_v = pltpu.make_async_copy(v_in, vv, load_sem.at[5])
    for load in (load_w, load_of, load_c, load_om, load_m, load_v):
        load.start()
    own_acts = []
    for b in range(4):
        load = pltpu.make_async_copy(
            a_in.at[:, pl.ds(column(x, b, c), 256)], acts.at[b, own_rows(t), :], own_sem.at[b]
        )
        load.start()
        own_acts.append(load)

    barrier = pltpu.get_barrier_semaphore()

    def greet(device):
        pl.semaphore_signal(barrier, inc=1, device_id=device, device_id_type=MESH)

    for i in range(1, 8):
        gx, gc = group(i)
        greet(at(gx, z, gc))
    greet(at(x, p, c))
    pl.when(inner == 1)(lambda: greet(at(x, q, c)))
    for i in range(1, 4):
        greet(rep_at((y + i) % 4, zh))
    greet(rep_at(y, 1 - zh))

    load_w.wait()
    wall[z] = wv[...].astype(BF16)
    load_of.wait()
    head = frag[0]
    picked = jnp.zeros((ROWS, HD), F32)
    for h in range(8):
        picked = jnp.where(head == h, wv[:, h * HD : (h + 1) * HD], picked)
    delta[...] = ofv[...] - picked

    pl.semaphore_wait(barrier, 12 + inner)

    def send_w(block, device, slot):
        remote(wall.at[block], wall.at[block], w_send.at[slot], w_recv.at[slot], device).start()

    @pl.when(inner == 0)
    def _():
        send_w(z, at(x, p, c), 0)

    @pl.when(inner == 1)
    def _():
        send_w(z, at(x, p, c), 1)
        send_w(z, at(x, q, c), 4)

    for i in (1, 3, 2):
        remote(c_in, cots.at[own_rows(t), :], c_send.at[i], c_recv.at[i], at(other_x(i), z, c)).start()
    remote(c_in, cots.at[own_rows(t), :], cf_send.at[0], cf_recv.at[0], at(x, z, 1 - c)).start()

    for b in order:

        @pl.loop(1, 8)
        def _(i):
            gx, gc = group(i)
            remote(
                a_in.at[:, pl.ds(column(gx, b, gc), 256)], acts.at[b, own_rows(t), :],
                a_send.at[0], a_recv.at[b], at(gx, z, gc),
            ).start()

    def chunk(index):
        return pl.ds(pl.multiple_of(index * 64, 64), 64)

    for i in range(1, 4):
        yy = (y + i) % 4
        remote(delta.at[chunk(yy), :], y_in.at[i], ys_send.at[i], ys_recv.at[i], rep_at(yy, zh)).start()

    for i in (1, 3, 2):
        src = cots.at[own_rows(from_x(i) * 2 + c), :]
        wait_bytes(src, c_recv.at[i])
        remote(src, src, cf_send.at[i], cf_recv.at[i], at(x, z, 1 - c)).start()

    @pl.when(inner == 1)
    def _():
        wait_bytes(wall.at[p], w_recv.at[0])
        send_w(p, at(x, q, c), 5)
        wait_bytes(wall.at[q], w_recv.at[4])
        send_w(q, at(x, p, c), 2)

    @pl.when(inner == 0)
    def _():
        wait_bytes(wall.at[p], w_recv.at[1])

    for i in range(1, 4):
        wait_bytes(y_in.at[i], ys_recv.at[i])
    zsum[...] = ((delta[chunk(y), :] + y_in[1]) + y_in[2]) + y_in[3]
    remote(zsum, z_in, zs_send.at[0], zs_recv.at[0], rep_at(y, 1 - zh)).start()

    load_c.wait()
    for i in range(4):
        wait_bytes(cots.at[own_rows(from_x(i) * 2 + 1 - c), :], cf_recv.at[i])

    def input_cotangent(b):
        @pl.loop(0, 4)
        def _(i):
            rows = pl.ds(pl.multiple_of(i * 256, 256), 256)
            got = lax.dot_general(
                cots[rows, :], wall[b], (((1,), (1,)), ((), ())), preferred_element_type=F32
            )
            dxs[b, rows, :] = (got * SCALE).astype(BF16)

        @pl.loop(1, 8)
        def _(i):
            gx, gc = group(i)
            remote(
                dxs.at[b, own_rows(gx * 2 + gc), :], dx_out.at[:, pl.ds(column(x, b, c), 256)],
                dx_send.at[0], dx_recv.at[0], at(gx, z, gc),
            ).start()

        pltpu.make_async_copy(
            dxs.at[b, own_rows(t), :], dx_out.at[:, pl.ds(column(x, b, c), 256)], dx_own.at[b]
        ).start()

    def gradient(k):
        b = order[k]
        pltpu.make_async_copy(
            a_in.at[:, pl.ds(column(x, b, c), 256)], acts.at[b, own_rows(t), :], own_sem.at[b]
        ).wait()
        wait_bytes(acts.at[b, pl.ds(0, 7 * TOK), :], a_recv.at[b])

        @pl.loop(0, 4)
        def _(i):
            cols = pl.ds(pl.multiple_of(i * 256, 256), 256)
            gblk[k, :, cols] = lax.dot_general(
                acts[b], cots[:, cols], (((0,), (0,)), ((), ())), preferred_element_type=F32
            )

    def send_g(k, land, recv, device):
        remote(gsend.at[k], land, g_send.at[k], recv, device).start()

    def outer_send(k):
        @pl.when(inner == 0)
        def _():
            gsend[k] = gblk[k].astype(BF16)
            send_g(k, g_oi.at[k], oi_recv.at[k], at(x, p, c))

    input_cotangent(z)
    gradient(0)
    outer_send(0)
    input_cotangent(p)
    gradient(1)
    outer_send(1)

    @pl.when(inner == 1)
    def _():
        wait_bytes(wall.at[r], w_recv.at[5])
        send_w(r, at(x, p, c), 3)

    @pl.when(inner == 0)
    def _():
        wait_bytes(wall.at[r], w_recv.at[2])

    wait_bytes(z_in, zs_recv.at[0])
    total[chunk(y), :] = zsum[...] + z_in[...]
    for i in range(1, 4):
        remote(
            total.at[chunk(y), :], total.at[chunk(y), :], yg_send.at[i], yg_recv.at[i],
            rep_at((y + i) % 4, zh),
        ).start()

    gradient(2)
    outer_send(2)

    @pl.when(inner == 1)
    def _():
        wait_bytes(g_oi.at[0], oi_recv.at[0])
        gsend[0] = (gblk[0] + g_oi[0].astype(F32)).astype(BF16)
        send_g(0, g_ii.at[0], ii_recv.at[0], at(x, q, c))

    input_cotangent(r + inner * (q - r))
    gradient(3)

    @pl.when(inner == 0)
    def _():
        wait_bytes(wall.at[q], w_recv.at[3])

    @pl.loop(0, 4)
    def _(i):
        rows = pl.ds(pl.multiple_of(i * 256, 256), 256)
        got = jnp.dot(acts[0, rows, :], wall[0], preferred_element_type=F32)
        for b in range(1, 4):
            got += jnp.dot(acts[b, rows, :], wall[b], preferred_element_type=F32)
        part[i] = got
        remote(
            part.at[i, own_rows(1 - c), :], part_in.at[i], pc_send.at[i], pc_recv.at[i], at(x, z, 1 - c)
        ).start()

    @pl.when(inner == 1)
    def _():
        wait_bytes(g_ii.at[0], ii_recv.at[0])
        gsend[1] = (gblk[1] + g_ii[0].astype(F32)).astype(BF16)
        send_g(1, g_io, io_recv.at[0], at(x, p, c))

    for i in (1, 3, 2):
        xx = other_x(i)
        wait_bytes(part_in.at[xx], pc_recv.at[xx])
        psend[i] = (part[xx, own_rows(c), :] + part_in[xx]).astype(BF16)
        remote(psend.at[i], p_in.at[i], px_send.at[i], px_recv.at[i], at(xx, z, c)).start()
    input_cotangent(q + inner * (r - q))

    @pl.when(inner == 1)
    def _():
        wait_bytes(g_oi.at[1], oi_recv.at[1])
        gsend[2] = (gblk[2] + g_oi[1].astype(F32)).astype(BF16)
        send_g(2, g_ii.at[1], ii_recv.at[1], at(x, q, c))

    for i in range(1, 4):
        wait_bytes(total.at[chunk((y + 4 - i) % 4), :], yg_recv.at[i])
    load_om.wait()
    average = total[...] / 8.0
    momentum = outer_beta * omv[...] + average
    fresh = ofv[...] - outer_rate * (average + outer_beta * momentum)
    omv[...] = momentum
    ofv[...] = fresh
    outs = [
        pltpu.make_async_copy(ofv, no_out, out_sem.at[0]),
        pltpu.make_async_copy(omv, nmom_out, out_sem.at[1]),
    ]
    for out in outs:
        out.start()

    @pl.when(inner == 0)
    def _():
        wait_bytes(g_io, io_recv.at[0])
        gblk[3] = gblk[3] + g_io[...].astype(F32)

    @pl.when(inner == 1)
    def _():
        wait_bytes(g_oi.at[2], oi_recv.at[2])
        wait_bytes(g_ii.at[1], ii_recv.at[1])
        gblk[3] = gblk[3] + g_oi[2].astype(F32) + g_ii[1].astype(F32)

    load_m.wait()
    load_v.wait()

    @pl.loop(0, 8)
    def _(i):
        rows = pl.ds(pl.multiple_of(i * 32, 32), 32)
        for h in range(8):
            cols = slice(h * HD, (h + 1) * HD)
            grad = gblk[3, rows, cols] * SCALE
            first = beta_first * mv[rows, cols] + (1.0 - beta_first) * grad
            second = beta_second * vv[rows, cols] + (1.0 - beta_second) * grad * grad
            local = wv[rows, cols]
            stepped = local - inner_rate * (first / (jnp.sqrt(second) + epsilon) + decay_rate * local)
            merged = mixing * stepped + (1.0 - mixing) * ofv[rows, :]
            mv[rows, cols] = first
            vv[rows, cols] = second
            wv[rows, cols] = jnp.where(head == h, merged, stepped)

    more = [
        pltpu.make_async_copy(wv, nw_out, out_sem.at[2]),
        pltpu.make_async_copy(mv, nm_out, out_sem.at[3]),
        pltpu.make_async_copy(vv, nv_out, out_sem.at[4]),
    ]
    for out in more:
        out.start()

    wait_bytes(part_in.at[x], pc_recv.at[x])
    for i in (1, 3, 2):
        wait_bytes(p_in.at[i], px_recv.at[i])
    got = part[x, own_rows(c), :] + part_in[x]
    for i in (1, 3, 2):
        got += p_in[i].astype(F32)
    pv[...] = (got * SCALE).astype(BF16)
    last = pltpu.make_async_copy(pv, proj_out, out_sem.at[5])
    last.start()

    @pl.when(inner == 0)
    def _():
        wait_bytes(wall.at[z], w_send.at[0])

    @pl.when(inner == 1)
    def _():
        for slot in range(1, 6):
            wait_bytes(wall.at[z], w_send.at[slot])

    for i in range(1, 4):
        wait_bytes(cots.at[own_rows(t), :], c_send.at[i])
        wait_bytes(psend.at[i], px_send.at[i])
        wait_bytes(delta.at[chunk(0), :], ys_send.at[i])
        wait_bytes(total.at[chunk(0), :], yg_send.at[i])
    wait_bytes(zsum, zs_send.at[0])
    for i in range(4):
        wait_bytes(cots.at[own_rows(t), :], cf_send.at[i])
        wait_bytes(part_in.at[i], pc_send.at[i])
    for k in range(3):
        wait_bytes(gsend.at[k], g_send.at[k])
    wait_bytes(dx_out.at[:, pl.ds(0, 28 * 256)], a_send.at[0])
    for out in (*outs, *more, last):
        out.wait()
    for b in range(4):
        wait_bytes(dxs.at[b, own_rows(t), :], dx_own.at[b])
    wait_bytes(dx_out.at[:, pl.ds(0, 28 * 256)], dx_send.at[0])
    wait_bytes(dx_out.at[:, pl.ds(0, 28 * 256)], dx_recv.at[0])


def finish_kernel(*refs):
    n = (len(refs) - 1) // 2
    sem = refs[-1]
    copies = [pltpu.make_async_copy(refs[i], refs[n + i], sem.at[i]) for i in range(n)]
    for copy in copies:
        copy.start()
    for copy in copies:
        copy.wait()


ANY = pl.BlockSpec(memory_space=pl.ANY)


def shards(activations, cotangent, weight, moment, variance, outer_frag, outer_mom, fragment):
    results = (
        ((TOK, KW), BF16),
        ((TOK, D), BF16),
        ((ROWS, KW), F32),
        ((ROWS, KW), F32),
        ((ROWS, KW), F32),
        ((ROWS, HD), F32),
        ((ROWS, HD), F32),
    )
    dma = pltpu.SemaphoreType.DMA
    outs = pl.pallas_call(
        step_kernel,
        out_shape=[pltpu.VMEM(shape, dtype) for shape, dtype in results],
        in_specs=[pl.BlockSpec(memory_space=pltpu.SMEM)] + [ANY] * 7,
        out_specs=[ANY] * 7,
        scratch_shapes=[
            pltpu.VMEM((4, 1024, 256), BF16),
            pltpu.VMEM((1024, KW), BF16),
            pltpu.VMEM((4, ROWS, KW), BF16),
            pltpu.VMEM((ROWS, KW), F32),
            pltpu.VMEM((ROWS, KW), F32),
            pltpu.VMEM((ROWS, KW), F32),
            pltpu.VMEM((ROWS, HD), F32),
            pltpu.VMEM((ROWS, HD), F32),
            pltpu.VMEM((ROWS, HD), F32),
            pltpu.VMEM((ROWS, HD), F32),
            pltpu.VMEM((4, ROWS, KW), F32),
            pltpu.VMEM((3, ROWS, KW), BF16),
            pltpu.VMEM((3, ROWS, KW), BF16),
            pltpu.VMEM((2, ROWS, KW), BF16),
            pltpu.VMEM((ROWS, KW), BF16),
            pltpu.VMEM((4, 256, KW), F32),
            pltpu.VMEM((4, TOK, KW), F32),
            pltpu.VMEM((4, TOK, KW), BF16),
            pltpu.VMEM((4, TOK, KW), BF16),
            pltpu.VMEM((TOK, KW), BF16),
            pltpu.VMEM((4, 1024, 256), BF16),
            pltpu.VMEM((4, 64, HD), F32),
            pltpu.VMEM((64, HD), F32),
            pltpu.VMEM((64, HD), F32),
            dma((6,)),
            dma((4,)),
            dma((6,)),
            dma((6,)),
            dma((6,)),
            dma((4,)),
            dma((4,)),
            dma((4,)),
            dma((4,)),
            dma((1,)),
            dma((4,)),
            dma((3,)),
            dma((3,)),
            dma((2,)),
            dma((1,)),
            dma((4,)),
            dma((4,)),
            dma((4,)),
            dma((4,)),
            dma((1,)),
            dma((1,)),
            dma((4,)),
            dma((4,)),
            dma((4,)),
            dma((1,)),
            dma((1,)),
            dma((4,)),
            dma((4,)),
        ],
        compiler_params=pltpu.CompilerParams(
            collective_id=0, has_side_effects=True, vmem_limit_bytes=40 * 2**20
        ),
    )(
        fragment,
        *(
            pltpu.with_memory_space_constraint(a, pltpu.HBM)
            for a in (
                activations[0], cotangent[0], weight[0], moment[0], variance[0], outer_frag, outer_mom
            )
        ),
    )
    outs = pl.pallas_call(
        finish_kernel,
        out_shape=[pltpu.HBM(shape, dtype) for shape, dtype in results],
        in_specs=[ANY] * 7,
        out_specs=[ANY] * 7,
        scratch_shapes=[dma((7,))],
        compiler_params=pltpu.CompilerParams(vmem_limit_bytes=2 * 2**20),
    )(*(pltpu.with_memory_space_constraint(a, pltpu.VMEM) for a in outs))
    return tuple(out[None] for out in outs[:5]) + tuple(outs[5:])


def solution(mesh):
    split = P("replica", "fsdp", None)
    return jax.shard_map(
        shards,
        mesh=mesh,
        in_specs=(split, split, split, split, split, P("fsdp", None), P("fsdp", None), P()),
        out_specs=(split, split, split, split, split, P("fsdp", None), P("fsdp", None)),
        check_vma=False,
    )
```

```python
import functools

import jax
import jax.numpy as jnp
from jax import lax
from jax.experimental import pallas as pl
from jax.experimental.pallas import tpu as pltpu
from jax.sharding import PartitionSpec as P

MESH = pl.DeviceIdType.MESH

D = 8192
HD = 128
KW = 1024
TOK = 128
ROWS = 256
SCALE = float(D) ** (-0.5)

beta_first = 0.9
beta_second = 0.95
inner_rate = 0.1
decay_rate = 0.1
epsilon = 1e-08
outer_rate = 0.7
outer_beta = 0.9
mixing = 0.5

F32 = jnp.float32
BF16 = jnp.bfloat16


def step_kernel(
    frag, a_in, c_in, w_in, m_in, v_in, of_in, om_in,
    proj_out, dx_out, nw_out, nm_out, nv_out, no_out, nmom_out,
    acts, cots, wall, wv, mv, vv, ofv, omv, delta, total, gblk, gsend, g_oi, g_ii, g_io,
    part, part_in, psend, p_in, dxs, y_in, zsum, z_in,
    load_sem, own_sem, w_send, w_recv, c_send, c_recv, cf_send, cf_recv,
    a_send, a_recv, g_send, oi_recv, ii_recv, io_recv, pc_send, pc_recv, px_send, px_recv,
    dx_send, dx_recv, dx_own, ys_send, ys_recv, zs_send, zs_recv, yg_send, yg_recv,
):
    rep = lax.axis_index("replica")
    fs = lax.axis_index("fsdp")
    y, zh = rep // 2, rep % 2
    x, z, c = fs // 8, (fs // 2) % 4, fs % 2
    t = x * 2 + c
    hi = z // 2
    inner = hi + (z % 2) - 2 * hi * (z % 2)
    p = z + 1 - 2 * (z % 2)
    q = 3 - z
    r = 3 - p

    def at(xx, zz, cc):
        return (rep, xx * 8 + zz * 2 + cc)

    def group(i):
        u = (t + i) % 8
        return u // 2, u % 2

    def other_x(i):
        return (x + i) % 4

    def rep_at(yy, hh):
        return (yy * 2 + hh, fs)

    def remote(src, dst, send, recv, device):
        return pltpu.make_async_remote_copy(
            src_ref=src, dst_ref=dst, send_sem=send, recv_sem=recv, device_id=device, device_id_type=MESH
        )

    def wait_bytes(ref, sem):
        pltpu.make_async_copy(ref, ref, sem).wait()

    order = (q + inner * (r - q), r + inner * (p - r), p + inner * (q - p), z)

    def block(b):
        return pl.ds(pl.multiple_of(b * 256, 256), 256)

    def column(xx, zz, cc):
        return pl.multiple_of(xx * 2048 + zz * 512 + cc * 256, 256)

    def own_rows(index):
        return pl.ds(pl.multiple_of(index * TOK, TOK), TOK)

    load_w = pltpu.make_async_copy(w_in, wv, load_sem.at[0])
    load_of = pltpu.make_async_copy(of_in, ofv, load_sem.at[1])
    load_c = pltpu.make_async_copy(c_in, cots.at[own_rows(t), :], load_sem.at[2])
    load_om = pltpu.make_async_copy(om_in, omv, load_sem.at[3])
    load_m = pltpu.make_async_copy(m_in, mv, load_sem.at[4])
    load_v = pltpu.make_async_copy(v_in, vv, load_sem.at[5])
    for load in (load_w, load_of, load_c, load_om, load_m, load_v):
        load.start()
    own_acts = []
    for b in range(4):
        load = pltpu.make_async_copy(
            a_in.at[:, pl.ds(column(x, b, c), 256)], acts.at[own_rows(t), block(b)], own_sem.at[b]
        )
        load.start()
        own_acts.append(load)

    barrier = pltpu.get_barrier_semaphore()

    def greet(device):
        pl.semaphore_signal(barrier, inc=1, device_id=device, device_id_type=MESH)

    for i in range(1, 8):
        gx, gc = group(i)
        greet(at(gx, z, gc))
    greet(at(x, p, c))
    pl.when(inner == 1)(lambda: greet(at(x, q, c)))
    for i in range(1, 4):
        greet(rep_at((y + i) % 4, zh))

    load_w.wait()
    wall[block(z), :] = wv[...].astype(BF16)
    load_of.wait()
    head = frag[0]
    picked = jnp.zeros((ROWS, HD), F32)
    for h in range(8):
        picked = jnp.where(head == h, wv[:, h * HD : (h + 1) * HD], picked)
    delta[...] = ofv[...] - picked

    pl.semaphore_wait(barrier, 11 + inner + zh)
    greet(rep_at(y, 1 - zh))

    def send_w(b, device, slot):
        remote(wall.at[block(b), :], wall.at[block(b), :], w_send.at[slot], w_recv.at[slot], device).start()

    @pl.when(inner == 0)
    def _():
        send_w(z, at(x, p, c), 0)

    @pl.when(inner == 1)
    def _():
        send_w(z, at(x, p, c), 1)
        send_w(z, at(x, q, c), 4)

    right, left = other_x(1), other_x(3)
    far = other_x(2)

    def half(index, side):
        return pl.ds(pl.multiple_of(index * TOK + side * 64, 64), 64)

    for slot, device in ((0, at(right, z, c)), (1, at(left, z, c))):
        remote(c_in, cots.at[own_rows(t), :], c_send.at[slot], c_recv.at[slot], device).start()
    remote(c_in, cots.at[own_rows(t), :], cf_send.at[0], cf_recv.at[0], at(x, z, 1 - c)).start()

    def send_acts(b):
        @pl.loop(1, 8)
        def _(i):
            gx, gc = group(i)
            remote(
                a_in.at[:, pl.ds(column(gx, b, gc), 256)], acts.at[own_rows(t), block(b)],
                a_send.at[0], a_recv.at[b], at(gx, z, gc),
            ).start()

    send_acts(order[0])

    def chunk(index):
        return pl.ds(pl.multiple_of(index * 64, 64), 64)

    for i in range(1, 4):
        yy = (y + i) % 4
        remote(delta.at[chunk(yy), :], y_in.at[i], ys_send.at[i], ys_recv.at[i], rep_at(yy, zh)).start()

    for slot, source, device in ((0, left, at(right, z, c)), (1, right, at(left, z, c))):
        rows = own_rows(source * 2 + c)
        part_rows = half(source * 2 + c, slot)
        wait_bytes(cots.at[rows, :], c_recv.at[slot])
        remote(
            cots.at[part_rows, :], cots.at[part_rows, :], c_send.at[2 + slot], c_recv.at[2 + slot], device
        ).start()
        remote(
            cots.at[rows, :], cots.at[rows, :], cf_send.at[1 + slot], cf_recv.at[1 + slot], at(x, z, 1 - c)
        ).start()
    send_acts(order[1])

    @pl.when(inner == 1)
    def _():
        wait_bytes(wall.at[block(p), :], w_recv.at[0])
        send_w(p, at(x, q, c), 5)
        wait_bytes(wall.at[block(q), :], w_recv.at[4])
        send_w(q, at(x, p, c), 2)

    @pl.when(inner == 0)
    def _():
        wait_bytes(wall.at[block(p), :], w_recv.at[1])

    def wait_acts(k):
        b = order[k]
        pltpu.make_async_copy(
            a_in.at[:, pl.ds(column(x, b, c), 256)], acts.at[own_rows(t), block(b)], own_sem.at[b]
        ).wait()
        wait_bytes(acts.at[pl.ds(0, 7 * TOK), block(b)], a_recv.at[b])

    wait_acts(0)
    send_acts(order[2])

    for i in range(1, 4):
        wait_bytes(y_in.at[i], ys_recv.at[i])
    zsum[...] = ((delta[chunk(y), :] + y_in[1]) + y_in[2]) + y_in[3]
    @pl.when(zh == 0)
    def _():
        pl.semaphore_wait(barrier, 1)

    remote(zsum, z_in, zs_send.at[0], zs_recv.at[0], rep_at(y, 1 - zh)).start()

    for slot in (0, 1):
        wait_bytes(cots.at[half(far * 2 + c, slot), :], c_recv.at[2 + slot])
    rows = own_rows(far * 2 + c)
    remote(cots.at[rows, :], cots.at[rows, :], cf_send.at[3], cf_recv.at[3], at(x, z, 1 - c)).start()
    load_c.wait()
    for slot, source in enumerate((x, left, right, far)):
        wait_bytes(cots.at[own_rows(source * 2 + 1 - c), :], cf_recv.at[slot])

    def input_cotangent(b):
        got = lax.dot_general(
            cots[...], wall[block(b), :], (((1,), (1,)), ((), ())), preferred_element_type=F32
        )
        dxs[b] = (got * SCALE).astype(BF16)

    def send_cotangent(b):
        @pl.loop(1, 8)
        def _(i):
            gx, gc = group(i)
            remote(
                dxs.at[b, own_rows(gx * 2 + gc), :], dx_out.at[:, pl.ds(column(x, b, c), 256)],
                dx_send.at[0], dx_recv.at[0], at(gx, z, gc),
            ).start()

        pltpu.make_async_copy(
            dxs.at[b, own_rows(t), :], dx_out.at[:, pl.ds(column(x, b, c), 256)], dx_own.at[b]
        ).start()

    def gradient(k):
        b = order[k]

        gblk[k] = lax.dot_general(
            acts[:, block(b)], cots[...], (((0,), (0,)), ((), ())), preferred_element_type=F32
        )

    def send_g(k, land, recv, device):
        remote(gsend.at[k], land, g_send.at[k], recv, device).start()

    def outer_send(k):
        @pl.when(inner == 0)
        def _():
            gsend[k] = gblk[k].astype(BF16)
            send_g(k, g_oi.at[k], oi_recv.at[k], at(x, p, c))

    gradient(0)
    outer_send(0)
    wait_acts(1)
    send_acts(order[3])
    gradient(1)
    outer_send(1)

    @pl.when(inner == 1)
    def _():
        wait_bytes(wall.at[block(r), :], w_recv.at[5])
        send_w(r, at(x, p, c), 3)

    @pl.when(inner == 0)
    def _():
        wait_bytes(wall.at[block(r), :], w_recv.at[2])

    input_cotangent(z)

    wait_bytes(z_in, zs_recv.at[0])
    total[chunk(y), :] = zsum[...] + z_in[...]
    for i in range(1, 4):
        remote(
            total.at[chunk(y), :], total.at[chunk(y), :], yg_send.at[i], yg_recv.at[i],
            rep_at((y + i) % 4, zh),
        ).start()

    wait_acts(2)
    send_cotangent(z)
    gradient(2)
    outer_send(2)
    third = r + inner * (q - r)
    fourth = q + inner * (r - q)
    input_cotangent(p)
    input_cotangent(third)

    @pl.when(inner == 1)
    def _():
        wait_bytes(g_oi.at[0], oi_recv.at[0])
        gsend[0] = (gblk[0] + g_oi[0].astype(F32)).astype(BF16)
        send_g(0, g_ii.at[0], ii_recv.at[0], at(x, q, c))

    wait_acts(3)
    send_cotangent(p)

    @pl.loop(0, 4)
    def _(i):
        got = jnp.dot(acts[block(i), block(z)], wall[block(z), :], preferred_element_type=F32)
        for b in (p, third):
            got += jnp.dot(acts[block(i), block(b)], wall[block(b), :], preferred_element_type=F32)
        part[i] = got

    @pl.when(inner == 0)
    def _():
        wait_bytes(wall.at[block(q), :], w_recv.at[3])

    def partial(xx):
        part[xx] += jnp.dot(
            acts[block(xx), block(fourth)], wall[block(fourth), :], preferred_element_type=F32
        )
        remote(
            part.at[xx, own_rows(1 - c), :], part_in.at[xx], pc_send.at[xx], pc_recv.at[xx], at(x, z, 1 - c)
        ).start()

    @pl.loop(0, 2)
    def _(i):
        partial((x + 2 - i) % 4)

    wait_bytes(part_in.at[far], pc_recv.at[far])
    psend[2] = (part[far, own_rows(c), :] + part_in[far]).astype(BF16)
    for slot, device in ((0, at(right, z, c)), (1, at(left, z, c))):
        rows = pl.ds(slot * 64, 64)
        remote(psend.at[2, rows, :], p_in.at[2, rows, :], px_send.at[2 + slot], px_recv.at[2 + slot], device).start()

    @pl.loop(0, 2)
    def _(i):
        partial((x + 3 + i) % 4)

    send_cotangent(third)
    gradient(3)
    input_cotangent(fourth)

    @pl.when(inner == 1)
    def _():
        wait_bytes(g_ii.at[0], ii_recv.at[0])
        gsend[1] = (gblk[1] + g_ii[0].astype(F32)).astype(BF16)
        send_g(1, g_io, io_recv.at[0], at(x, p, c))
        wait_bytes(g_oi.at[1], oi_recv.at[1])
        gsend[2] = (gblk[2] + g_oi[1].astype(F32)).astype(BF16)
        send_g(2, g_ii.at[1], ii_recv.at[1], at(x, q, c))

    for slot, target in ((0, right), (1, left)):
        rows = pl.ds(slot * 64, 64)
        wait_bytes(part_in.at[target], pc_recv.at[target])
        wait_bytes(p_in.at[2, rows, :], px_recv.at[2 + slot])
        both = part[target, own_rows(c), :] + part_in[target]
        psend[slot] = both.astype(BF16)
        psend[slot, rows, :] = (both[slot * 64 : slot * 64 + 64] + p_in[2, rows, :].astype(F32)).astype(BF16)
        remote(psend.at[slot], p_in.at[slot], px_send.at[slot], px_recv.at[slot], at(target, z, c)).start()

    send_cotangent(fourth)

    for i in range(1, 4):
        wait_bytes(total.at[chunk((y + 4 - i) % 4), :], yg_recv.at[i])
    load_om.wait()
    average = total[...] / 8.0
    momentum = outer_beta * omv[...] + average
    fresh = ofv[...] - outer_rate * (average + outer_beta * momentum)
    nmom_out[...] = momentum
    no_out[...] = fresh

    @pl.when(inner == 0)
    def _():
        wait_bytes(g_io, io_recv.at[0])
        gblk[3] = gblk[3] + g_io[...].astype(F32)

    @pl.when(inner == 1)
    def _():
        wait_bytes(g_oi.at[2], oi_recv.at[2])
        wait_bytes(g_ii.at[1], ii_recv.at[1])
        gblk[3] = gblk[3] + g_oi[2].astype(F32) + g_ii[1].astype(F32)

    load_m.wait()
    load_v.wait()

    @pl.loop(0, 8)
    def _(i):
        rows = pl.ds(pl.multiple_of(i * 32, 32), 32)
        for h in range(8):
            cols = slice(h * HD, (h + 1) * HD)
            grad = gblk[3, rows, cols] * SCALE
            first = beta_first * mv[rows, cols] + (1.0 - beta_first) * grad
            second = beta_second * vv[rows, cols] + (1.0 - beta_second) * grad * grad
            local = wv[rows, cols]
            stepped = local - inner_rate * (first / (jnp.sqrt(second) + epsilon) + decay_rate * local)
            merged = mixing * stepped + (1.0 - mixing) * no_out[rows, :]
            nm_out[rows, cols] = first
            nv_out[rows, cols] = second
            nw_out[rows, cols] = jnp.where(head == h, merged, stepped)

    wait_bytes(part_in.at[x], pc_recv.at[x])
    got = part[x, own_rows(c), :] + part_in[x]
    for slot in (0, 1):
        wait_bytes(p_in.at[slot], px_recv.at[slot])
        got += p_in[slot].astype(F32)
    proj_out[...] = (got * SCALE).astype(BF16)

    @pl.when(inner == 0)
    def _():
        wait_bytes(wall.at[block(z), :], w_send.at[0])

    @pl.when(inner == 1)
    def _():
        for slot in range(1, 6):
            wait_bytes(wall.at[block(z), :], w_send.at[slot])

    for i in range(1, 4):
        wait_bytes(delta.at[chunk(0), :], ys_send.at[i])
        wait_bytes(total.at[chunk(0), :], yg_send.at[i])
    wait_bytes(zsum, zs_send.at[0])
    for slot in (0, 1):
        wait_bytes(cots.at[own_rows(t), :], c_send.at[slot])
        wait_bytes(cots.at[half(t, 0), :], c_send.at[2 + slot])
        wait_bytes(psend.at[slot], px_send.at[slot])
        wait_bytes(psend.at[2, pl.ds(0, 64), :], px_send.at[2 + slot])
    for i in range(4):
        wait_bytes(cots.at[own_rows(t), :], cf_send.at[i])
        wait_bytes(part_in.at[i], pc_send.at[i])
    for k in range(3):
        wait_bytes(gsend.at[k], g_send.at[k])
    wait_bytes(dx_out.at[:, pl.ds(0, 28 * 256)], a_send.at[0])
    for b in range(4):
        wait_bytes(dxs.at[b, own_rows(t), :], dx_own.at[b])
    wait_bytes(dx_out.at[:, pl.ds(0, 28 * 256)], dx_send.at[0])
    wait_bytes(dx_out.at[:, pl.ds(0, 28 * 256)], dx_recv.at[0])


def finish_kernel(*refs):
    n = (len(refs) - 1) // 2
    sem = refs[-1]
    copies = [pltpu.make_async_copy(refs[i], refs[n + i], sem.at[i]) for i in range(n)]
    for copy in copies:
        copy.start()
    for copy in copies:
        copy.wait()


ANY = pl.BlockSpec(memory_space=pl.ANY)


def shards(activations, cotangent, weight, moment, variance, outer_frag, outer_mom, fragment):
    results = (
        ((TOK, KW), BF16),
        ((TOK, D), BF16),
        ((ROWS, KW), F32),
        ((ROWS, KW), F32),
        ((ROWS, KW), F32),
        ((ROWS, HD), F32),
        ((ROWS, HD), F32),
    )
    dma = pltpu.SemaphoreType.DMA
    outs = pl.pallas_call(
        step_kernel,
        out_shape=[pltpu.VMEM(shape, dtype) for shape, dtype in results],
        in_specs=[pl.BlockSpec(memory_space=pltpu.SMEM)] + [ANY] * 7,
        out_specs=[pl.BlockSpec(memory_space=pltpu.VMEM)] * 7,
        scratch_shapes=[
            pltpu.VMEM((1024, 1024), BF16),
            pltpu.VMEM((1024, KW), BF16),
            pltpu.VMEM((1024, KW), BF16),
            pltpu.VMEM((ROWS, KW), F32),
            pltpu.VMEM((ROWS, KW), F32),
            pltpu.VMEM((ROWS, KW), F32),
            pltpu.VMEM((ROWS, HD), F32),
            pltpu.VMEM((ROWS, HD), F32),
            pltpu.VMEM((ROWS, HD), F32),
            pltpu.VMEM((ROWS, HD), F32),
            pltpu.VMEM((4, ROWS, KW), F32),
            pltpu.VMEM((3, ROWS, KW), BF16),
            pltpu.VMEM((3, ROWS, KW), BF16),
            pltpu.VMEM((2, ROWS, KW), BF16),
            pltpu.VMEM((ROWS, KW), BF16),
            pltpu.VMEM((4, 256, KW), F32),
            pltpu.VMEM((4, TOK, KW), F32),
            pltpu.VMEM((3, TOK, KW), BF16),
            pltpu.VMEM((3, TOK, KW), BF16),
            pltpu.VMEM((4, 1024, 256), BF16),
            pltpu.VMEM((4, 64, HD), F32),
            pltpu.VMEM((64, HD), F32),
            pltpu.VMEM((64, HD), F32),
            dma((6,)),
            dma((4,)),
            dma((6,)),
            dma((6,)),
            dma((4,)),
            dma((4,)),
            dma((4,)),
            dma((4,)),
            dma((1,)),
            dma((4,)),
            dma((3,)),
            dma((3,)),
            dma((2,)),
            dma((1,)),
            dma((4,)),
            dma((4,)),
            dma((4,)),
            dma((4,)),
            dma((1,)),
            dma((1,)),
            dma((4,)),
            dma((4,)),
            dma((4,)),
            dma((1,)),
            dma((1,)),
            dma((4,)),
            dma((4,)),
        ],
        compiler_params=pltpu.CompilerParams(
            collective_id=0, has_side_effects=True, vmem_limit_bytes=40 * 2**20
        ),
    )(
        fragment,
        *(
            pltpu.with_memory_space_constraint(a, pltpu.HBM)
            for a in (
                activations[0], cotangent[0], weight[0], moment[0], variance[0], outer_frag, outer_mom
            )
        ),
    )
    outs = pl.pallas_call(
        finish_kernel,
        out_shape=[pltpu.HBM(shape, dtype) for shape, dtype in results],
        in_specs=[ANY] * 7,
        out_specs=[ANY] * 7,
        scratch_shapes=[dma((7,))],
        compiler_params=pltpu.CompilerParams(vmem_limit_bytes=2 * 2**20),
    )(*(pltpu.with_memory_space_constraint(a, pltpu.VMEM) for a in outs))
    return tuple(out[None] for out in outs[:5]) + tuple(outs[5:])


def solution(mesh):
    split = P("replica", "fsdp", None)
    return jax.shard_map(
        shards,
        mesh=mesh,
        in_specs=(split, split, split, split, split, P("fsdp", None), P("fsdp", None), P()),
        out_specs=(split, split, split, split, split, P("fsdp", None), P("fsdp", None)),
        check_vma=False,
    )
```

```python
import functools

import jax
import jax.numpy as jnp
from jax import lax
from jax.experimental import pallas as pl
from jax.experimental.pallas import tpu as pltpu
from jax.sharding import PartitionSpec as P

MESH = pl.DeviceIdType.MESH

D = 8192
HD = 128
KW = 1024
TOK = 128
ROWS = 256
SCALE = float(D) ** (-0.5)

beta_first = 0.9
beta_second = 0.95
inner_rate = 0.1
decay_rate = 0.1
epsilon = 1e-08
outer_rate = 0.7
outer_beta = 0.9
mixing = 0.5

F32 = jnp.float32
BF16 = jnp.bfloat16


def step_kernel(
    frag, a_in, c_in, w_in, m_in, v_in, of_in, om_in,
    proj_out, dx_out, nw_out, nm_out, nv_out, no_out, nmom_out,
    acts, cots, wall, wv, mv, vv, ofv, omv, delta, total, gblk, gsend, g_oi, g_ii, g_io,
    part, part_in, psend, p_in, dxs, y_in, zsum, z_in,
    load_sem, own_sem, w_send, w_recv, c_send, c_recv, cf_send, cf_recv,
    a_send, a_recv, g_send, oi_recv, ii_recv, io_recv, pc_send, pc_recv, px_send, px_recv,
    dx_send, dx_recv, dx_own, ys_send, ys_recv, zs_send, zs_recv, yg_send, yg_recv,
):
    rep = lax.axis_index("replica")
    fs = lax.axis_index("fsdp")
    y, zh = rep // 2, rep % 2
    x, z, c = fs // 8, (fs // 2) % 4, fs % 2
    t = x * 2 + c
    hi = z // 2
    inner = hi + (z % 2) - 2 * hi * (z % 2)
    p = z + 1 - 2 * (z % 2)
    q = 3 - z
    r = 3 - p

    def at(xx, zz, cc):
        return (rep, xx * 8 + zz * 2 + cc)

    def group(i):
        u = (t + i) % 8
        return u // 2, u % 2

    def other_x(i):
        return (x + i) % 4

    def rep_at(yy, hh):
        return (yy * 2 + hh, fs)

    def remote(src, dst, send, recv, device):
        return pltpu.make_async_remote_copy(
            src_ref=src, dst_ref=dst, send_sem=send, recv_sem=recv, device_id=device, device_id_type=MESH
        )

    def wait_bytes(ref, sem):
        pltpu.make_async_copy(ref, ref, sem).wait()

    order = (q + inner * (r - q), r + inner * (p - r), p + inner * (q - p), z)

    def block(b):
        return pl.ds(pl.multiple_of(b * 256, 256), 256)

    def column(xx, zz, cc):
        return pl.multiple_of(xx * 2048 + zz * 512 + cc * 256, 256)

    def own_rows(index):
        return pl.ds(pl.multiple_of(index * TOK, TOK), TOK)

    barrier = pltpu.get_barrier_semaphore()

    def greet(device):
        pl.semaphore_signal(barrier, inc=1, device_id=device, device_id_type=MESH)

    for i in range(1, 8):
        gx, gc = group(i)
        greet(at(gx, z, gc))
    greet(at(x, p, c))
    pl.when(inner == 1)(lambda: greet(at(x, q, c)))
    for i in range(1, 4):
        greet(rep_at((y + i) % 4, zh))

    load_w = pltpu.make_async_copy(w_in, wv, load_sem.at[0])
    load_of = pltpu.make_async_copy(of_in, ofv, load_sem.at[1])
    load_c = pltpu.make_async_copy(c_in, cots.at[own_rows(t), :], load_sem.at[2])
    load_om = pltpu.make_async_copy(om_in, omv, load_sem.at[3])
    load_m = pltpu.make_async_copy(m_in, mv, load_sem.at[4])
    load_v = pltpu.make_async_copy(v_in, vv, load_sem.at[5])
    for load in (load_w, load_of, load_c, load_om, load_m, load_v):
        load.start()
    for b in range(4):
        load = pltpu.make_async_copy(
            a_in.at[:, pl.ds(column(x, b, c), 256)], acts.at[own_rows(t), block(b)], own_sem.at[b]
        )
        load.start()

    load_w.wait()
    wall[block(z), :] = wv[...].astype(BF16)
    load_of.wait()
    head = frag[0]
    picked = jnp.zeros((ROWS, HD), F32)
    for h in range(8):
        picked = jnp.where(head == h, wv[:, h * HD : (h + 1) * HD], picked)
    delta[...] = ofv[...] - picked

    pl.semaphore_wait(barrier, 11 + inner + zh)
    greet(rep_at(y, 1 - zh))

    def send_w(b, device, slot):
        remote(wall.at[block(b), :], wall.at[block(b), :], w_send.at[slot], w_recv.at[slot], device).start()

    @pl.when(inner == 0)
    def _():
        send_w(z, at(x, p, c), 0)

    @pl.when(inner == 1)
    def _():
        send_w(z, at(x, p, c), 1)
        send_w(z, at(x, q, c), 4)

    right, left = other_x(1), other_x(3)
    far = other_x(2)

    def half(index, side):
        return pl.ds(pl.multiple_of(index * TOK + side * 64, 64), 64)

    load_c.wait()
    mine = cots.at[own_rows(t), :]

    for slot, device in ((0, at(right, z, c)), (1, at(left, z, c))):
        remote(mine, mine, c_send.at[slot], c_recv.at[slot], device).start()
    remote(mine, mine, cf_send.at[0], cf_recv.at[0], at(x, z, 1 - c)).start()

    def send_acts(b, first=1, last=8):
        @pl.loop(first, last)
        def _(i):
            gx, gc = group(i)
            remote(
                a_in.at[:, pl.ds(column(gx, b, gc), 256)], acts.at[own_rows(t), block(b)],
                a_send.at[0], a_recv.at[b], at(gx, z, gc),
            ).start()

    send_acts(order[0], 3, 6)

    def chunk(index):
        return pl.ds(pl.multiple_of(index * 64, 64), 64)

    for i in range(1, 4):
        yy = (y + i) % 4
        remote(delta.at[chunk(yy), :], y_in.at[i], ys_send.at[i], ys_recv.at[i], rep_at(yy, zh)).start()

    for slot, source, device in ((0, left, at(right, z, c)), (1, right, at(left, z, c))):
        rows = own_rows(source * 2 + c)
        part_rows = half(source * 2 + c, slot)
        wait_bytes(cots.at[rows, :], c_recv.at[slot])
        remote(
            cots.at[part_rows, :], cots.at[part_rows, :], c_send.at[2 + slot], c_recv.at[2 + slot], device
        ).start()
        remote(
            cots.at[rows, :], cots.at[rows, :], cf_send.at[1 + slot], cf_recv.at[1 + slot], at(x, z, 1 - c)
        ).start()
    send_acts(order[0], 1, 3)
    send_acts(order[0], 6, 8)
    send_acts(order[1])

    @pl.when(inner == 1)
    def _():
        wait_bytes(wall.at[block(p), :], w_recv.at[0])
        send_w(p, at(x, q, c), 5)
        wait_bytes(wall.at[block(q), :], w_recv.at[4])
        send_w(q, at(x, p, c), 2)

    @pl.when(inner == 0)
    def _():
        wait_bytes(wall.at[block(p), :], w_recv.at[1])

    def wait_acts(k):
        b = order[k]
        pltpu.make_async_copy(
            a_in.at[:, pl.ds(column(x, b, c), 256)], acts.at[own_rows(t), block(b)], own_sem.at[b]
        ).wait()
        wait_bytes(acts.at[pl.ds(0, 7 * TOK), block(b)], a_recv.at[b])

    wait_acts(0)
    send_acts(order[2])

    for i in range(1, 4):
        wait_bytes(y_in.at[i], ys_recv.at[i])
    zsum[...] = ((delta[chunk(y), :] + y_in[1]) + y_in[2]) + y_in[3]
    @pl.when(zh == 0)
    def _():
        pl.semaphore_wait(barrier, 1)

    remote(zsum, z_in, zs_send.at[0], zs_recv.at[0], rep_at(y, 1 - zh)).start()

    for slot in (0, 1):
        wait_bytes(cots.at[half(far * 2 + c, slot), :], c_recv.at[2 + slot])
    rows = own_rows(far * 2 + c)
    remote(cots.at[rows, :], cots.at[rows, :], cf_send.at[3], cf_recv.at[3], at(x, z, 1 - c)).start()
    for slot, source in enumerate((x, left, right, far)):
        wait_bytes(cots.at[own_rows(source * 2 + 1 - c), :], cf_recv.at[slot])

    def input_cotangent(b):
        got = lax.dot_general(
            cots[...], wall[block(b), :], (((1,), (1,)), ((), ())), preferred_element_type=F32
        )
        dxs[b] = (got * SCALE).astype(BF16)

    def send_cotangent(b):
        @pl.loop(1, 8)
        def _(i):
            gx, gc = group(i)
            remote(
                dxs.at[b, own_rows(gx * 2 + gc), :], dx_out.at[:, pl.ds(column(x, b, c), 256)],
                dx_send.at[0], dx_recv.at[0], at(gx, z, gc),
            ).start()

        pltpu.make_async_copy(
            dxs.at[b, own_rows(t), :], dx_out.at[:, pl.ds(column(x, b, c), 256)], dx_own.at[b]
        ).start()

    def gradient(k):
        b = order[k]

        gblk[k] = lax.dot_general(
            acts[:, block(b)], cots[...], (((0,), (0,)), ((), ())), preferred_element_type=F32
        )

    def send_g(k, land, recv, device):
        remote(gsend.at[k], land, g_send.at[k], recv, device).start()

    def outer_send(k):
        @pl.when(inner == 0)
        def _():
            gsend[k] = gblk[k].astype(BF16)
            send_g(k, g_oi.at[k], oi_recv.at[k], at(x, p, c))

    gradient(0)
    outer_send(0)
    wait_acts(1)
    send_acts(order[3])
    gradient(1)
    outer_send(1)

    @pl.when(inner == 1)
    def _():
        wait_bytes(wall.at[block(r), :], w_recv.at[5])
        send_w(r, at(x, p, c), 3)

    @pl.when(inner == 0)
    def _():
        wait_bytes(wall.at[block(r), :], w_recv.at[2])

    input_cotangent(z)

    wait_bytes(z_in, zs_recv.at[0])
    total[chunk(y), :] = zsum[...] + z_in[...]
    for i in range(1, 4):
        remote(
            total.at[chunk(y), :], total.at[chunk(y), :], yg_send.at[i], yg_recv.at[i],
            rep_at((y + i) % 4, zh),
        ).start()

    wait_acts(2)
    send_cotangent(z)
    gradient(2)
    outer_send(2)
    third = r + inner * (q - r)
    fourth = q + inner * (r - q)
    input_cotangent(p)
    input_cotangent(third)

    @pl.when(inner == 1)
    def _():
        wait_bytes(g_oi.at[0], oi_recv.at[0])
        gsend[0] = (gblk[0] + g_oi[0].astype(F32)).astype(BF16)
        send_g(0, g_ii.at[0], ii_recv.at[0], at(x, q, c))

    wait_acts(3)
    send_cotangent(p)

    @pl.loop(0, 4)
    def _(i):
        got = jnp.dot(acts[block(i), block(z)], wall[block(z), :], preferred_element_type=F32)
        for b in (p, third):
            got += jnp.dot(acts[block(i), block(b)], wall[block(b), :], preferred_element_type=F32)
        part[i] = got

    @pl.when(inner == 0)
    def _():
        wait_bytes(wall.at[block(q), :], w_recv.at[3])

    def partial(xx):
        part[xx] += jnp.dot(
            acts[block(xx), block(fourth)], wall[block(fourth), :], preferred_element_type=F32
        )
        remote(
            part.at[xx, own_rows(1 - c), :], part_in.at[xx], pc_send.at[xx], pc_recv.at[xx], at(x, z, 1 - c)
        ).start()

    @pl.loop(0, 2)
    def _(i):
        partial((x + 2 - i) % 4)

    wait_bytes(part_in.at[far], pc_recv.at[far])
    psend[2] = (part[far, own_rows(c), :] + part_in[far]).astype(BF16)
    for slot, device in ((0, at(right, z, c)), (1, at(left, z, c))):
        rows = pl.ds(slot * 64, 64)
        remote(psend.at[2, rows, :], p_in.at[2, rows, :], px_send.at[2 + slot], px_recv.at[2 + slot], device).start()

    @pl.loop(0, 2)
    def _(i):
        partial((x + 3 + i) % 4)

    send_cotangent(third)
    gradient(3)
    input_cotangent(fourth)

    @pl.when(inner == 1)
    def _():
        wait_bytes(g_ii.at[0], ii_recv.at[0])
        gsend[1] = (gblk[1] + g_ii[0].astype(F32)).astype(BF16)
        send_g(1, g_io, io_recv.at[0], at(x, p, c))
        wait_bytes(g_oi.at[1], oi_recv.at[1])
        gsend[2] = (gblk[2] + g_oi[1].astype(F32)).astype(BF16)
        send_g(2, g_ii.at[1], ii_recv.at[1], at(x, q, c))

    for slot, target in ((0, right), (1, left)):
        rows = pl.ds(slot * 64, 64)
        wait_bytes(part_in.at[target], pc_recv.at[target])
        wait_bytes(p_in.at[2, rows, :], px_recv.at[2 + slot])
        both = part[target, own_rows(c), :] + part_in[target]
        psend[slot] = both.astype(BF16)
        psend[slot, rows, :] = (both[slot * 64 : slot * 64 + 64] + p_in[2, rows, :].astype(F32)).astype(BF16)
        remote(psend.at[slot], p_in.at[slot], px_send.at[slot], px_recv.at[slot], at(target, z, c)).start()

    send_cotangent(fourth)

    for i in range(1, 4):
        wait_bytes(total.at[chunk((y + 4 - i) % 4), :], yg_recv.at[i])
    load_om.wait()
    average = total[...] / 8.0
    momentum = outer_beta * omv[...] + average
    fresh = ofv[...] - outer_rate * (average + outer_beta * momentum)
    nmom_out[...] = momentum
    no_out[...] = fresh

    @pl.when(inner == 0)
    def _():
        wait_bytes(g_io, io_recv.at[0])
        gblk[3] = gblk[3] + g_io[...].astype(F32)

    @pl.when(inner == 1)
    def _():
        wait_bytes(g_oi.at[2], oi_recv.at[2])
        wait_bytes(g_ii.at[1], ii_recv.at[1])
        gblk[3] = gblk[3] + g_oi[2].astype(F32) + g_ii[1].astype(F32)

    load_m.wait()
    load_v.wait()

    @pl.loop(0, 8)
    def _(i):
        rows = pl.ds(pl.multiple_of(i * 32, 32), 32)
        for h in range(8):
            cols = slice(h * HD, (h + 1) * HD)
            grad = gblk[3, rows, cols] * SCALE
            first = beta_first * mv[rows, cols] + (1.0 - beta_first) * grad
            second = beta_second * vv[rows, cols] + (1.0 - beta_second) * grad * grad
            local = wv[rows, cols]
            stepped = local - inner_rate * (first / (jnp.sqrt(second) + epsilon) + decay_rate * local)
            merged = mixing * stepped + (1.0 - mixing) * no_out[rows, :]
            nm_out[rows, cols] = first
            nv_out[rows, cols] = second
            nw_out[rows, cols] = jnp.where(head == h, merged, stepped)

    wait_bytes(part_in.at[x], pc_recv.at[x])
    got = part[x, own_rows(c), :] + part_in[x]
    for slot in (0, 1):
        wait_bytes(p_in.at[slot], px_recv.at[slot])
        got += p_in[slot].astype(F32)
    proj_out[...] = (got * SCALE).astype(BF16)

    @pl.when(inner == 0)
    def _():
        wait_bytes(wall.at[block(z), :], w_send.at[0])

    @pl.when(inner == 1)
    def _():
        for slot in range(1, 6):
            wait_bytes(wall.at[block(z), :], w_send.at[slot])

    for i in range(1, 4):
        wait_bytes(delta.at[chunk(0), :], ys_send.at[i])
        wait_bytes(total.at[chunk(0), :], yg_send.at[i])
    wait_bytes(zsum, zs_send.at[0])
    for slot in (0, 1):
        wait_bytes(cots.at[own_rows(t), :], c_send.at[slot])
        wait_bytes(cots.at[half(t, 0), :], c_send.at[2 + slot])
        wait_bytes(psend.at[slot], px_send.at[slot])
        wait_bytes(psend.at[2, pl.ds(0, 64), :], px_send.at[2 + slot])
    for i in range(4):
        wait_bytes(cots.at[own_rows(t), :], cf_send.at[i])
        wait_bytes(part_in.at[i], pc_send.at[i])
    for k in range(3):
        wait_bytes(gsend.at[k], g_send.at[k])
    wait_bytes(dx_out.at[:, pl.ds(0, 28 * 256)], a_send.at[0])
    for b in range(4):
        wait_bytes(dxs.at[b, own_rows(t), :], dx_own.at[b])
    wait_bytes(dx_out.at[:, pl.ds(0, 28 * 256)], dx_send.at[0])
    wait_bytes(dx_out.at[:, pl.ds(0, 28 * 256)], dx_recv.at[0])


def finish_kernel(*refs):
    n = (len(refs) - 1) // 2
    sem = refs[-1]
    copies = [pltpu.make_async_copy(refs[i], refs[n + i], sem.at[i]) for i in range(n)]
    for copy in copies:
        copy.start()
    for copy in copies:
        copy.wait()


ANY = pl.BlockSpec(memory_space=pl.ANY)


def shards(activations, cotangent, weight, moment, variance, outer_frag, outer_mom, fragment):
    results = (
        ((TOK, KW), BF16),
        ((TOK, D), BF16),
        ((ROWS, KW), F32),
        ((ROWS, KW), F32),
        ((ROWS, KW), F32),
        ((ROWS, HD), F32),
        ((ROWS, HD), F32),
    )
    dma = pltpu.SemaphoreType.DMA
    outs = pl.pallas_call(
        step_kernel,
        out_shape=[pltpu.VMEM(shape, dtype) for shape, dtype in results],
        in_specs=[pl.BlockSpec(memory_space=pltpu.SMEM)] + [ANY] * 7,
        out_specs=[pl.BlockSpec(memory_space=pltpu.VMEM)] * 7,
        scratch_shapes=[
            pltpu.VMEM((1024, 1024), BF16),
            pltpu.VMEM((1024, KW), BF16),
            pltpu.VMEM((1024, KW), BF16),
            pltpu.VMEM((ROWS, KW), F32),
            pltpu.VMEM((ROWS, KW), F32),
            pltpu.VMEM((ROWS, KW), F32),
            pltpu.VMEM((ROWS, HD), F32),
            pltpu.VMEM((ROWS, HD), F32),
            pltpu.VMEM((ROWS, HD), F32),
            pltpu.VMEM((ROWS, HD), F32),
            pltpu.VMEM((4, ROWS, KW), F32),
            pltpu.VMEM((3, ROWS, KW), BF16),
            pltpu.VMEM((3, ROWS, KW), BF16),
            pltpu.VMEM((2, ROWS, KW), BF16),
            pltpu.VMEM((ROWS, KW), BF16),
            pltpu.VMEM((4, 256, KW), F32),
            pltpu.VMEM((4, TOK, KW), F32),
            pltpu.VMEM((3, TOK, KW), BF16),
            pltpu.VMEM((3, TOK, KW), BF16),
            pltpu.VMEM((4, 1024, 256), BF16),
            pltpu.VMEM((4, 64, HD), F32),
            pltpu.VMEM((64, HD), F32),
            pltpu.VMEM((64, HD), F32),
            dma((6,)),
            dma((4,)),
            dma((6,)),
            dma((6,)),
            dma((4,)),
            dma((4,)),
            dma((4,)),
            dma((4,)),
            dma((1,)),
            dma((4,)),
            dma((3,)),
            dma((3,)),
            dma((2,)),
            dma((1,)),
            dma((4,)),
            dma((4,)),
            dma((4,)),
            dma((4,)),
            dma((1,)),
            dma((1,)),
            dma((4,)),
            dma((4,)),
            dma((4,)),
            dma((1,)),
            dma((1,)),
            dma((4,)),
            dma((4,)),
        ],
        compiler_params=pltpu.CompilerParams(
            collective_id=0, has_side_effects=True, vmem_limit_bytes=40 * 2**20
        ),
    )(
        fragment,
        *(
            pltpu.with_memory_space_constraint(a, pltpu.HBM)
            for a in (
                activations[0], cotangent[0], weight[0], moment[0], variance[0], outer_frag, outer_mom
            )
        ),
    )
    outs = pl.pallas_call(
        finish_kernel,
        out_shape=[pltpu.HBM(shape, dtype) for shape, dtype in results],
        in_specs=[ANY] * 7,
        out_specs=[ANY] * 7,
        scratch_shapes=[dma((7,))],
        compiler_params=pltpu.CompilerParams(vmem_limit_bytes=2 * 2**20),
    )(*(pltpu.with_memory_space_constraint(a, pltpu.VMEM) for a in outs))
    return tuple(out[None] for out in outs[:5]) + tuple(outs[5:])


def solution(mesh):
    split = P("replica", "fsdp", None)
    return jax.shard_map(
        shards,
        mesh=mesh,
        in_specs=(split, split, split, split, split, P("fsdp", None), P("fsdp", None), P()),
        out_specs=(split, split, split, split, split, P("fsdp", None), P("fsdp", None)),
        check_vma=False,
    )
```
